256 devices in a mesh: series: 32 (over z_hi, x, core), tm: 8 (over z_lo, y).
Axes of the slice: x: 4, y: 4, z: 8 (z_hi: 4, z_lo: 2; z = z_hi * 2 + z_lo), core: 2. Of those that a mesh axis runs over, the one named last changes fastest.
Arguments:
- series_data: bfloat16 [128, 1024, 1024], P('series', 'tm'), may hold values from -6 to 6
- group_ids: int32 [128], replicated, may hold values from 0 to 95, never falling along the last dimension, each value on 1 to 4 neighbouring positions
- group_query: bfloat16 [1024, 512], replicated, may hold values from -1.5 to 1.5
- group_key: bfloat16 [1024, 512], replicated, may hold values from -1.5 to 1.5
- group_value: bfloat16 [1024, 512], replicated, may hold values from -0.1875 to 0.1875
- group_out: bfloat16 [512, 1024], replicated, may hold values from -0.25 to 0.25
- time_query: bfloat16 [1024, 512], replicated, may hold values from -1.5 to 1.5
- time_key: bfloat16 [1024, 512], replicated, may hold values from -1.5 to 1.5
- time_value: bfloat16 [1024, 512], replicated, may hold values from -0.1875 to 0.1875
- time_out: bfloat16 [512, 1024], replicated, may hold values from -0.25 to 0.25
Outputs:
- layer_out: bfloat16 [128, 1024, 1024], P('series', 'tm')
The draws below stay inside these ranges and needn't reach their ends.
Inputs may be any that keep to these rules, and one draw needn't show every extreme that they name: `group_ids`: group numbers never fall along the series; each group holds 1 to 4 series, one exactly 4.
All inputs are finite; a program needn't handle non-finite values.
Results may differ from the reference program's by a relative error of at most 0.0065.
Values may be sent and summed in bfloat16 or wider, within the bound.
No kernel may reach another device: no remote copies, remote signals or barrier semaphores. Data moves between devices by JAX's collectives and lax.ppermute only.
A program may use at most 128 MiB of HBM per device.

```python
import math
import jax
import jax.numpy as jnp
import numpy as np
from jax import lax

D = 1024
HEADS = 8
HEAD_DIM = 64
MOST = 4
INNER = 512
SERIES = 128
PATCHES = 1024
GROUPS = 96


def own_part(key):
    return jax.random.normal(key, (D, HEADS * HEAD_DIM), jnp.float32) / math.sqrt(D)


def draw_group_query(key, part):
    key = jax.random.fold_in(key, 11)
    matrix = own_part(key)
    return jnp.clip(matrix, -1.5, 1.5).astype(jnp.bfloat16)


def draw_group_key(key, part):
    key = jax.random.fold_in(key, 12)
    matrix = own_part(key)
    return jnp.clip(matrix, -1.5, 1.5).astype(jnp.bfloat16)


def draw_time_query(key, part):
    key = jax.random.fold_in(key, 13)
    matrix = own_part(key)
    return jnp.clip(matrix, -1.5, 1.5).astype(jnp.bfloat16)


def draw_time_key(key, part):
    key = jax.random.fold_in(key, 14)
    matrix = own_part(key)
    return jnp.clip(matrix, -1.5, 1.5).astype(jnp.bfloat16)


def shard_levels(key, shape, cuts, smallest, top_value):
    level = 1.0
    for dim, shards_of in cuts:
        draws = jax.random.uniform(jax.random.fold_in(jax.random.fold_in(key, 6), dim), (shards_of,), jnp.float32, smallest / len(cuts), top_value / len(cuts))
        level = level * jnp.repeat(jnp.exp(draws), shape[dim] // shards_of).reshape((-1,) + (1,) * (len(shape) - 1 - dim))
    return level


def split_up(amount, total, limit, slope):
    loads = [(1 << 20) // math.isqrt(grade ** slope) + 1 for grade in range(2, amount + 1)]
    spare, counts = total - limit - (amount - 1), [1] * (amount - 1)
    while spare > 0:
        movable = [i for i in range(amount - 1) if counts[i] < limit]
        mass, budget = sum([loads[i] for i in movable]), spare
        for i in movable:
            extra = min(limit - counts[i], max(1, budget * loads[i] // mass), spare)
            counts[i] = counts[i] + extra
            spare = spare - extra
    return np.array([limit] + counts)


def ragged_sizes(own_key, count, total, bound, slope):
    if count == 2:
        one = jax.random.randint(own_key, (), max(1, total - bound), min(bound, total - 1) + 1)
        return jnp.stack([one, total - one])
    lengths = jnp.asarray(split_up(count, total, bound, slope), jnp.int32)
    pairs = (count - 1) // 2
    giver, receiver = lengths[1:1 + 2 * pairs:2], lengths[2:2 + 2 * pairs:2]
    room = jnp.minimum(giver - 1, bound - receiver)
    moved = jax.random.randint(jax.random.fold_in(own_key, 1), (pairs,), 0, 1 << 20) % (room + 1)
    lengths = lengths.at[1:1 + 2 * pairs:2].set(giver - moved).at[2:2 + 2 * pairs:2].set(receiver + moved)
    return lengths[jax.random.permutation(jax.random.fold_in(own_key, 2), count)]


def bell_draw(stream_key, dims, spread, bound, cuts=(), held_as=jnp.bfloat16):
    entries = jax.random.normal(stream_key, dims, jnp.float32) * spread
    if len(cuts) > 0:
        entries = shard_levels(stream_key, dims, cuts, -0.22, 0.18) * entries
    return jnp.clip(entries, min=-bound, max=bound).astype(held_as)


def setup_inputs(seed: int = 0) -> dict:
    key_list = jax.random.split(jax.random.key(seed), 11)
    return {
        "series_data": bell_draw(key_list[0], (SERIES, PATCHES, D), 1.0, 6.0, ((0, 32), (1, 8))),
        "group_ids": jnp.searchsorted(jnp.cumsum(ragged_sizes(key_list[1], GROUPS, SERIES, MOST, 2)), jnp.arange(SERIES), side="right").astype(jnp.int32),
        "group_query": draw_group_query(jax.random.fold_in(key_list[10], 71), 0),
        "group_key": draw_group_key(jax.random.fold_in(key_list[10], 71), 0),
        "group_value": bell_draw(key_list[4], (D, INNER), D ** -0.5, 0.1875),
        "group_out": bell_draw(key_list[5], (INNER, D), INNER ** -0.5, 0.25),
        "time_query": draw_time_query(jax.random.fold_in(key_list[10], 71), 0),
        "time_key": draw_time_key(jax.random.fold_in(key_list[10], 71), 0),
        "time_value": bell_draw(key_list[8], (D, INNER), D ** -0.5, 0.1875),
        "time_out": bell_draw(key_list[9], (INNER, D), INNER ** -0.5, 0.25),
    }


def rms_norm(values):
    wide = values.astype(jnp.float32)
    return wide * lax.rsqrt(lax.optimization_barrier(jnp.mean(wide * wide, axis=-1, keepdims=True)) + 1e-06)

def project(normed, weight):
    leading = normed.shape[:-1]
    result = jnp.dot(normed.reshape(-1, normed.shape[-1]), weight, preferred_element_type=jnp.float32)
    return result.reshape(leading + (weight.shape[1],))

def rotate(values, positions):
    halfway = values.shape[-1] // 2
    freqs = 10000.0 ** (-jnp.arange(halfway, dtype=jnp.float32) / halfway)
    angles = positions.astype(jnp.float32)[:, None] * freqs[None, :]
    cosine = jnp.cos(angles)[None, :, None, :]
    sine = jnp.sin(angles)[None, :, None, :]
    first = values[..., :halfway]
    second = values[..., halfway:]
    return jnp.concatenate([first * cosine - second * sine, first * sine + second * cosine], axis=-1)

def group_attend(queries, keys, values, query_ids, key_ids):
    rows, spots, inner = queries.shape
    count = keys.shape[0]
    query_h = queries.reshape(rows, spots, HEADS, HEAD_DIM).astype(jnp.float32)
    key_h = keys.reshape(count, spots, HEADS, HEAD_DIM).astype(jnp.float32)
    value_h = values.reshape(count, spots, HEADS, HEAD_DIM).astype(jnp.float32)
    scores = jnp.einsum('sphd,jphd->phsj', query_h, key_h) * HEAD_DIM ** (-0.5)
    allowed = query_ids[:, None] == key_ids[None, :]
    scores = jnp.where(allowed[None, None], scores, -1e+30)
    row_top = lax.optimization_barrier(jnp.max(scores, axis=-1, keepdims=True))
    weights = jnp.where(allowed[None, None], jnp.exp(scores - row_top), 0.0)
    totals = lax.optimization_barrier(jnp.sum(weights, axis=-1))
    rounded = weights.astype(jnp.bfloat16).astype(jnp.float32)
    mixed = jnp.einsum('phsj,jphd->sphd', rounded, value_h)
    mixed = mixed / jnp.transpose(totals, (2, 0, 1))[..., None]
    return mixed.reshape(rows, spots, inner).astype(jnp.bfloat16)

def time_attend(pieces):
    query_a, key_a, value_a = pieces
    scores = jnp.einsum('qhd,khd->hqk', query_a.astype(jnp.float32), key_a.astype(jnp.float32)) * HEAD_DIM ** (-0.5)
    row_top = lax.optimization_barrier(jnp.max(scores, axis=-1, keepdims=True))
    weights = jnp.exp(scores - row_top)
    totals = lax.optimization_barrier(jnp.sum(weights, axis=-1))
    rounded = weights.astype(jnp.bfloat16).astype(jnp.float32)
    mixed = jnp.einsum('hqk,khd->qhd', rounded, value_a.astype(jnp.float32))
    mixed = mixed / jnp.transpose(totals, (1, 0))[..., None]
    return mixed.astype(jnp.bfloat16)

def reference(series_data, group_ids, group_query, group_key, group_value, group_out, time_query, time_key, time_value, time_out):
    series_count, patch_count, feature = series_data.shape
    inner = HEADS * HEAD_DIM
    normed_g = rms_norm(series_data).astype(jnp.bfloat16)
    query_g = project(normed_g, group_query).astype(jnp.bfloat16)
    key_g = project(normed_g, group_key).astype(jnp.bfloat16)
    value_g = project(normed_g, group_value).astype(jnp.bfloat16)
    blocks = patch_count // 8

    def regroup(values):
        return jnp.transpose(values.reshape(series_count, blocks, 8, inner), (1, 0, 2, 3))

    def one_block(pieces):
        return group_attend(pieces[0], pieces[1], pieces[2], group_ids, group_ids)
    mixed_g = lax.map(one_block, (regroup(query_g), regroup(key_g), regroup(value_g)))
    mixed_g = jnp.transpose(mixed_g, (1, 0, 2, 3)).reshape(series_count, patch_count, inner)
    middle = (series_data.astype(jnp.float32) + project(mixed_g, group_out)).astype(jnp.bfloat16)
    normed_t = rms_norm(middle).astype(jnp.bfloat16)
    positions = jnp.arange(patch_count, dtype=jnp.int32)
    query_t = rotate(project(normed_t, time_query).reshape(series_count, patch_count, HEADS, HEAD_DIM), positions).astype(jnp.bfloat16)
    key_t = rotate(project(normed_t, time_key).reshape(series_count, patch_count, HEADS, HEAD_DIM), positions).astype(jnp.bfloat16)
    value_t = project(normed_t, time_value).astype(jnp.bfloat16).reshape(series_count, patch_count, HEADS, HEAD_DIM)
    mixed_t = lax.map(time_attend, (query_t, key_t, value_t)).reshape(series_count, patch_count, inner)
    return (middle.astype(jnp.float32) + project(mixed_t, time_out)).astype(jnp.bfloat16)
```

```python
import functools

import jax
import jax.numpy as jnp
from jax import lax
from jax.experimental import pallas as pl
from jax.experimental.pallas import tpu as pltpu
from jax.sharding import Mesh, PartitionSpec as P

HEADS = 8
HEAD_DIM = 64
REACH = 3
BF16 = jnp.bfloat16
F32 = jnp.float32
SERIES = ("zh", "x", "core")
TIME = ("zl", "y")
VMEM_LIMIT = 48 * 1024 * 1024
VMEM = pl.BlockSpec(memory_space=pltpu.VMEM)
ANY = pl.BlockSpec(memory_space=pl.ANY)
SMEM = pl.BlockSpec(memory_space=pltpu.SMEM)


def dot(a, b):
    return jnp.dot(a, b, preferred_element_type=F32)


def normed(values):
    wide = values.astype(F32)
    return (wide * lax.rsqrt(jnp.mean(wide * wide, axis=-1, keepdims=True) + 1e-06)).astype(BF16)


def own_kernel(x_ref, b_ref, wq_ref, wk_ref, wv_ref, q_ref, k_ref, v_ref, kb_ref, vb_ref):
    rows = x_ref.shape[0]
    for at in range(0, rows, 256):
        part = pl.ds(at, 256)
        norm = normed(x_ref[part])
        q_ref[part] = (dot(norm, wq_ref[...]) * HEAD_DIM ** -0.5).astype(BF16)
        k_ref[part] = dot(norm, wk_ref[...]).astype(BF16)
        v_ref[part] = dot(norm, wv_ref[...]).astype(BF16)
    norm = normed(b_ref[...])
    kb_ref[...] = dot(norm, wk_ref[...]).astype(BF16)
    vb_ref[...] = dot(norm, wv_ref[...]).astype(BF16)


def turn(values, cosine, sine):
    lane = lax.broadcasted_iota(jnp.int32, cosine.shape, 1)
    low = lane % HEAD_DIM < HEAD_DIM // 2
    out = []
    for at in range(0, values.shape[1], 128):
        v = values[:, at : at + 128]
        swapped = jnp.where(low, pltpu.roll(v, 96, 1), pltpu.roll(v, 32, 1))
        out.append(v * cosine + swapped * sine)
    return jnp.concatenate(out, axis=1)


def middle_kernel(
    info_ref, x_hbm, q_hbm, k_hbm, v_hbm, kb_hbm, vb_hbm, ha_hbm, wk_hbm, wv_hbm, wo_hbm,
    tq_hbm, tk_hbm, tv_hbm, cos_ref, sin_ref,
    mid_ref, send_ref,
    x_ref, q_ref, kbuf, vbuf, ha_ref, wk_ref, wv_ref, wo_ref, tq_ref, tk_ref, tv_ref, mix_ref, sems,
):
    pt = cos_ref.shape[0]
    base_a = pl.multiple_of(info_ref[0] * pt, pt)
    base_b = pl.multiple_of(info_ref[1] * pt, pt)
    halo = REACH * pt
    own = x_ref.shape[0]
    pairs = [
        (ha_hbm, ha_ref), (wk_hbm, wk_ref), (wv_hbm, wv_ref),
        (k_hbm, kbuf.at[pl.ds(halo, own)]), (kb_hbm, kbuf.at[pl.ds(base_b, halo)]),
        (v_hbm, vbuf.at[pl.ds(halo, own)]), (vb_hbm, vbuf.at[pl.ds(base_b, halo)]),
        (q_hbm, q_ref), (x_hbm, x_ref), (wo_hbm, wo_ref),
        (tq_hbm, tq_ref), (tk_hbm, tk_ref), (tv_hbm, tv_ref),
    ]
    copies = [pltpu.make_async_copy(a, b, sems.at[i]) for i, (a, b) in enumerate(pairs)]
    for c in copies:
        c.start()
    inner = q_ref.shape[1]
    for c in copies[:3]:
        c.wait()
    norm = normed(ha_ref[...])
    kbuf[pl.ds(base_a, halo)] = dot(norm, wk_ref[...]).astype(BF16)
    vbuf[pl.ds(base_a, halo)] = dot(norm, wv_ref[...]).astype(BF16)
    for c in copies[3:8]:
        c.wait()
    row = lax.broadcasted_iota(jnp.int32, (inner, 128), 0)
    col = lax.broadcasted_iota(jnp.int32, (inner, 128), 1)
    gather = (row // HEAD_DIM == col).astype(BF16)
    row = lax.broadcasted_iota(jnp.int32, (128, inner), 0)
    col = lax.broadcasted_iota(jnp.int32, (128, inner), 1)
    spread = (col // HEAD_DIM == row).astype(BF16)
    span = 2 * REACH + 1
    for s in range(own // pt):
        q = q_ref[s * pt : (s + 1) * pt]
        prods = [q * kbuf[(s + j) * pt : (s + j + 1) * pt] for j in range(span)]
        scores = dot(jnp.concatenate(prods, axis=0), gather)
        mine = info_ref[2 + s + REACH]
        parts = []
        for j in range(span):
            same = info_ref[2 + s + j] == mine
            parts.append(jnp.where(same, scores[j * pt : (j + 1) * pt], -1e30))
        top = functools.reduce(jnp.maximum, parts)
        weights = [jnp.exp(p - top) for p in parts]
        inverse = 1.0 / functools.reduce(jnp.add, weights)
        high = inverse.astype(BF16)
        rest = (inverse - high.astype(F32)).astype(BF16)
        wide = dot(jnp.concatenate([w.astype(BF16) for w in weights] + [high, rest], axis=0), spread)
        total = jnp.zeros((pt, inner), F32)
        for j in range(span):
            total += wide[j * pt : (j + 1) * pt] * vbuf[(s + j) * pt : (s + j + 1) * pt].astype(F32)
        total *= wide[span * pt : (span + 1) * pt] + wide[(span + 1) * pt :]
        mix_ref[s * pt : (s + 1) * pt] = total.astype(BF16)
    for c in copies[8:]:
        c.wait()
    cosine, sine = cos_ref[...], sin_ref[...]
    half = inner // 2
    step = 2 * pt
    cosine = jnp.concatenate([cosine, cosine], axis=0)
    sine = jnp.concatenate([sine, sine], axis=0)
    for at in range(0, own, step):
        part = pl.ds(at, step)
        mid = (x_ref[part].astype(F32) + dot(mix_ref[part], wo_ref[...])).astype(BF16)
        mid_ref[part] = mid
        norm = normed(mid)
        q = (turn(dot(norm, tq_ref[...]), cosine, sine) * HEAD_DIM ** -0.5).astype(BF16)
        k = turn(dot(norm, tk_ref[...]), cosine, sine).astype(BF16)
        v = dot(norm, tv_ref[...]).astype(BF16)
        for i in range(2):
            s = at // pt + i
            for h in range(2):
                for n, a in enumerate((q, k, v)):
                    send_ref[2 * s + h, :, n * half : (n + 1) * half] = a[
                        i * pt : (i + 1) * pt, h * half : (h + 1) * half
                    ]


def time_kernel(in_ref, out_ref):
    blocks, pt, width = in_ref.shape
    half = width // 3
    k = in_ref[:, :, half : 2 * half].reshape(blocks * pt, half)
    v = in_ref[:, :, 2 * half :].reshape(blocks * pt, half)
    lane = lax.broadcasted_iota(jnp.int32, (1, half), 1)
    step = 2
    for at in range(0, blocks, step):
        q = in_ref[at : at + step, :, :half].reshape(step * pt, half)
        out = jnp.zeros((step * pt, half), F32)
        for h in range(half // HEAD_DIM):
            keep = lane // HEAD_DIM == h
            scores = lax.dot_general(
                jnp.where(keep, q, jnp.zeros_like(q)), k, (((1,), (1,)), ((), ())),
                preferred_element_type=F32,
            )
            weights = jnp.exp(scores - jnp.max(scores, axis=-1, keepdims=True))
            total = jnp.sum(weights, axis=-1, keepdims=True)
            out = jnp.where(keep, dot(weights.astype(BF16), v) / total, out)
        out_ref[at : at + step] = out.reshape(step, pt, half).astype(BF16)


def out_kernel(mixed_ref, mid_ref, wo_ref, out_ref):
    blocks, pt, half = mixed_ref.shape
    for s in range(blocks // 2):
        part = pl.ds(s * pt, pt)
        mixed = jnp.concatenate([mixed_ref[2 * s], mixed_ref[2 * s + 1]], axis=1)
        out_ref[part] = (mid_ref[part].astype(F32) + dot(mixed, wo_ref[...])).astype(BF16)


def params():
    return pltpu.CompilerParams(vmem_limit_bytes=VMEM_LIMIT)


def cost(flops, moved):
    return pl.CostEstimate(flops=flops, bytes_accessed=moved, transcendentals=0)


def shape(*dims):
    return jax.ShapeDtypeStruct(dims, BF16)


def on_device(
    series_data, group_ids, group_query, group_key, group_value, group_out,
    time_query, time_key, time_value, time_out,
):
    s_dev, pt, feature = series_data.shape
    inner = group_query.shape[1]
    rows, halo = s_dev * pt, REACH * pt
    core = lax.axis_index("core")
    place = lax.axis_index(SERIES)
    count = lax.axis_size(SERIES)
    shift = s_dev - REACH
    x = series_data.reshape(rows, feature)
    to_pair = lax.dynamic_slice_in_dim(x, jnp.where(core == 0, shift * pt, 0), halo)
    to_far = lax.dynamic_slice_in_dim(x, jnp.where(core == 0, 0, shift * pt), halo)
    far = []
    for i in range(1, count - 1, 2):
        far += [(i, i + 1), (i + 1, i)]
    halo_a = lax.ppermute(to_far, SERIES, far)
    halo_b = lax.ppermute(to_pair, "core", [(0, 1), (1, 0)])

    positions = lax.axis_index(TIME) * pt + jnp.arange(pt, dtype=jnp.int32)
    halfway = HEAD_DIM // 2
    freqs = 10000.0 ** (-jnp.arange(halfway, dtype=F32) / halfway)
    angles = positions.astype(F32)[:, None] * freqs[None, :]
    cosine, sine = jnp.cos(angles), jnp.sin(angles)
    cosine = jnp.concatenate([cosine] * 4, axis=1)
    sine = jnp.concatenate([-sine, sine, -sine, sine], axis=1)
    padded = jnp.pad(group_ids, (REACH, REACH), constant_values=-1)
    window = lax.dynamic_slice_in_dim(padded, place * s_dev, s_dev + 2 * REACH)
    right = s_dev + REACH
    base = jnp.stack([jnp.where(core == 0, 0, right), jnp.where(core == 0, right, 0)])
    info = jnp.concatenate([base.astype(jnp.int32), window])

    q, k, v, kb, vb = pl.pallas_call(
        own_kernel,
        out_shape=[shape(rows, inner)] * 3 + [shape(halo, inner)] * 2,
        in_specs=[VMEM] * 5,
        out_specs=[VMEM] * 5,
        compiler_params=params(),
        cost_estimate=cost(2 * feature * inner * (3 * rows + 2 * halo), 8 << 20),
        name="own",
    )(x, halo_b, group_query, group_key, group_value)

    mid, send = pl.pallas_call(
        middle_kernel,
        out_shape=[shape(rows, feature), shape(2 * s_dev, pt, 3 * inner // 2)],
        in_specs=[SMEM] + [ANY] * 13 + [VMEM] * 2,
        out_specs=[VMEM] * 2,
        scratch_shapes=[
            pltpu.VMEM((rows, feature), BF16),
            pltpu.VMEM((rows, inner), BF16),
            pltpu.VMEM((rows + 2 * halo, inner), BF16),
            pltpu.VMEM((rows + 2 * halo, inner), BF16),
            pltpu.VMEM((halo, feature), BF16),
            pltpu.VMEM((feature, inner), BF16),
            pltpu.VMEM((feature, inner), BF16),
            pltpu.VMEM((inner, feature), BF16),
            pltpu.VMEM((feature, inner), BF16),
            pltpu.VMEM((feature, inner), BF16),
            pltpu.VMEM((feature, inner), BF16),
            pltpu.VMEM((rows, inner), BF16),
            pltpu.SemaphoreType.DMA((13,)),
        ],
        compiler_params=params(),
        cost_estimate=cost(2 * feature * inner * (5 * rows + 2 * halo), 14 << 20),
        name="middle",
    )(info, x, q, k, v, kb, vb, halo_a, group_key, group_value, group_out,
      time_query, time_key, time_value, cosine, sine)

    got = lax.all_to_all(send, TIME, split_axis=0, concat_axis=0, tiled=True)
    mixed = pl.pallas_call(
        time_kernel,
        out_shape=shape(2 * s_dev, pt, inner // 2),
        in_specs=[VMEM],
        out_specs=VMEM,
        compiler_params=params(),
        cost_estimate=cost(8 << 30, 2 << 20),
        name="time",
    )(got)
    back = lax.all_to_all(mixed, TIME, split_axis=0, concat_axis=0, tiled=True)
    out = pl.pallas_call(
        out_kernel,
        out_shape=shape(rows, feature),
        in_specs=[VMEM] * 3,
        out_specs=VMEM,
        compiler_params=params(),
        cost_estimate=cost(2 * feature * inner * rows, 4 << 20),
        name="out",
    )(back, mid, time_out)
    return out.reshape(s_dev, pt, feature)


def solution(mesh):
    names = ("zh", "x", "core", "zl", "y")
    fine = Mesh(mesh.devices.reshape(4, 4, 2, 2, 4), names)
    whole = P(SERIES, TIME, None)
    placed = (whole,) + (P(),) * 9
    return jax.shard_map(
        on_device, mesh=fine, in_specs=placed, out_specs=whole, check_vma=False
    )
```

```python
import functools

import jax
import jax.numpy as jnp
from jax import lax
from jax.experimental import pallas as pl
from jax.experimental.pallas import tpu as pltpu
from jax.sharding import Mesh, PartitionSpec as P

HEADS = 8
HEAD_DIM = 64
REACH = 3
BF16 = jnp.bfloat16
F32 = jnp.float32
SERIES = ("zh", "x", "core")
TIME = ("zl", "y")
VMEM = pl.BlockSpec(memory_space=pltpu.VMEM)
ANY = pl.BlockSpec(memory_space=pl.ANY)
HBM = pl.BlockSpec(memory_space=pltpu.HBM)
SMEM = pl.BlockSpec(memory_space=pltpu.SMEM)


def dot(a, b):
    return jnp.dot(a, b, preferred_element_type=F32)


def normed(values):
    wide = values.astype(F32)
    return (wide * lax.rsqrt(jnp.mean(wide * wide, axis=-1, keepdims=True) + 1e-06)).astype(BF16)


def cut_kernel(x_hbm, far_ref, sems):
    rows, halo = x_hbm.shape[0], far_ref.shape[0]
    pt = rows - halo
    first = pl.multiple_of(jnp.where(lax.axis_index("core") == 0, 0, pt), pt)
    step = halo // sems.shape[0]
    copies = [
        pltpu.make_async_copy(
            x_hbm.at[pl.ds(first + i * step, step)], far_ref.at[pl.ds(i * step, step)], sems.at[i]
        )
        for i in range(sems.shape[0])
    ]
    for c in copies:
        c.start()
    for c in copies:
        c.wait()


def head_maps(inner):
    row = lax.broadcasted_iota(jnp.int32, (inner, 128), 0)
    col = lax.broadcasted_iota(jnp.int32, (inner, 128), 1)
    gather = (row // HEAD_DIM == col).astype(BF16)
    row = lax.broadcasted_iota(jnp.int32, (128, inner), 0)
    col = lax.broadcasted_iota(jnp.int32, (128, inner), 1)
    return gather, (col // HEAD_DIM == row).astype(BF16)


def attend(q, keys, values, same, gather, spread):
    pt = q.shape[0]
    scores = dot(jnp.concatenate([q * k for k in keys], axis=0), gather)
    parts = [jnp.where(m, scores[j * pt : (j + 1) * pt], -1e30) for j, m in enumerate(same)]
    top = functools.reduce(jnp.maximum, parts)
    weights = [jnp.exp(p - top) for p in parts]
    inverse = 1.0 / functools.reduce(jnp.add, weights)
    high = inverse.astype(BF16)
    low = (inverse - high.astype(F32)).astype(BF16)
    wide = dot(jnp.concatenate([w.astype(BF16) for w in weights] + [high, low], axis=0), spread)
    total = jnp.zeros(q.shape, F32)
    for j, v in enumerate(values):
        total += wide[j * pt : (j + 1) * pt] * v.astype(F32)
    last = len(keys) * pt
    return (total * (wide[last : last + pt] + wide[last + pt :])).astype(BF16)


def turn(values, cosine, sine):
    lane = lax.broadcasted_iota(jnp.int32, cosine.shape, 1)
    low = lane % HEAD_DIM < HEAD_DIM // 2
    out = []
    for at in range(0, values.shape[1], 128):
        v = values[:, at : at + 128]
        swapped = jnp.where(low, pltpu.roll(v, 96, 1), pltpu.roll(v, 32, 1))
        out.append(v * cosine + swapped * sine)
    return jnp.concatenate(out, axis=1)


def advance(x, mixed, wo_ref, tq_ref, tk_ref, tv_ref, cosine, sine):
    mid = (x.astype(F32) + dot(mixed, wo_ref[...])).astype(BF16)
    norm = normed(mid)
    q = (turn(dot(norm, tq_ref[...]), cosine, sine) * HEAD_DIM ** -0.5).astype(BF16)
    k = turn(dot(norm, tk_ref[...]), cosine, sine).astype(BF16)
    return mid, q, k, dot(norm, tv_ref[...]).astype(BF16)


def fetch(sources, targets, sems):
    copies = []
    for i, (a, b) in enumerate(zip(sources, targets)):
        rows = a.shape[0] // 2
        copies.append([
            pltpu.make_async_copy(a.at[pl.ds(n * rows, rows)], b.at[pl.ds(n * rows, rows)], sems.at[i, n])
            for n in range(2)
        ])
    for c in copies:
        c[0].start()
        c[1].start()

    def wait(*which):
        for i in which:
            copies[i][0].wait()
            copies[i][1].wait()

    return wait


def own_kernel(
    ids_ref, x_ref, pair_ref, wq_hbm, wk_hbm, wv_hbm, wo_hbm, tq_hbm, tk_hbm, tv_hbm, cos_ref, sin_ref,
    q_ref, k_ref, v_ref, mid_ref, send_ref, wk_ref, wv_ref, wo_ref, tq_ref, tk_ref, tv_ref,
    mix_ref, wq_ref, sems,
):
    wait = fetch(
        (wq_hbm, wk_hbm, wv_hbm, wo_hbm, tq_hbm, tk_hbm, tv_hbm),
        (wq_ref, wk_ref, wv_ref, wo_ref, tq_ref, tk_ref, tv_ref), sems,
    )
    pt, rows, inner = cos_ref.shape[0], x_ref.shape[0], q_ref.shape[1]
    own, halo = rows // pt, REACH * pt
    first = lax.axis_index("core") == 0
    own_spot = jnp.where(first, 0, REACH)
    pair_row = pl.multiple_of(jnp.where(first, rows, 0), pt)
    own_row = pl.multiple_of(own_spot * pt, pt)
    step = 2 * pt
    wait(0, 1, 2)
    for at in range(0, rows, step):
        norm = normed(x_ref[pl.ds(at, step)])
        part = pl.ds(pl.multiple_of(own_row + at, pt), step)
        q_ref[pl.ds(at, step)] = (dot(norm, wq_ref[...]) * HEAD_DIM ** -0.5).astype(BF16)
        k_ref[part] = dot(norm, wk_ref[...]).astype(BF16)
        v_ref[part] = dot(norm, wv_ref[...]).astype(BF16)
    source = pl.multiple_of(jnp.where(first, 0, pt), pt)
    norm = normed(pair_ref[pl.ds(source, halo)])
    k_ref[pl.ds(pair_row, halo)] = dot(norm, wk_ref[...]).astype(BF16)
    v_ref[pl.ds(pair_row, halo)] = dot(norm, wv_ref[...]).astype(BF16)
    gather, spread = head_maps(inner)
    span, count = REACH + 1, ids_ref.shape[0]
    place = lax.axis_index(SERIES) * own
    for s in range(own):
        index = place + s
        mine = ids_ref[index]
        back = jnp.int32(0)
        for j in range(1, span):
            back += ((ids_ref[jnp.maximum(index - j, 0)] == mine) & (index >= j)).astype(jnp.int32)
        start = jnp.clip(own_spot + s - back, 0, REACH)
        spots = [pl.ds(pl.multiple_of((start + j) * pt, pt), pt) for j in range(span)]
        others = [place - own_spot + start + j for j in range(span)]
        same = [
            (ids_ref[jnp.clip(o, 0, count - 1)] == mine) & (o >= 0) & (o < count) for o in others
        ]
        mix_ref[s * pt : (s + 1) * pt] = attend(
            q_ref[s * pt : (s + 1) * pt], [k_ref[p] for p in spots], [v_ref[p] for p in spots],
            same, gather, spread,
        )
    wait(3, 4, 5, 6)
    half = inner // 2
    cosine = jnp.concatenate([cos_ref[...]] * 2, axis=0)
    sine = jnp.concatenate([sin_ref[...]] * 2, axis=0)
    for at in range(0, rows, step):
        part = pl.ds(at, step)
        mid, q, k, v = advance(x_ref[part], mix_ref[part], wo_ref, tq_ref, tk_ref, tv_ref, cosine, sine)
        mid_ref[part] = mid
        for i in range(2):
            for h in range(2):
                for n, a in enumerate((q, k, v)):
                    send_ref[2 * (at // pt + i) + h, :, n * half : (n + 1) * half] = a[
                        i * pt : (i + 1) * pt, h * half : (h + 1) * half
                    ]


def fix_kernel(
    ids_ref, far_ref, x_ref, q_ref, k_ref, v_ref, wk_ref, wv_ref, wo_ref, tq_ref, tk_ref, tv_ref,
    cos_ref, sin_ref, mid_in, send_in,
    mid_out, send_out,
    fk_ref, fv_ref, mix_ref, mid_ref, send_ref, sems,
):
    del mid_in, send_in
    pt, rows, inner = cos_ref.shape[0], x_ref.shape[0], q_ref.shape[1]
    own, count = rows // pt, ids_ref.shape[0]
    first = lax.axis_index("core") == 0
    place = lax.axis_index(SERIES) * own
    edge = jnp.where(first, place, place + own - 1)
    way = jnp.where(first, -1, 1)
    mine = ids_ref[edge]

    def run(start, step, most):
        size = jnp.int32(0)
        for j in range(most):
            at = start + j * step
            size += ((at >= 0) & (at < count) & (ids_ref[jnp.clip(at, 0, count - 1)] == mine)).astype(jnp.int32)
        return size

    far = run(edge + way, way, REACH)
    near = run(edge, -way, REACH)
    half, halo = inner // 2, REACH * pt
    base = pl.multiple_of(jnp.where(first, 0, pt), pt)
    lows = [pl.multiple_of(jnp.where(first, j, REACH - 1 - j) * pt, pt) for j in range(REACH)]

    def finish(low, size):
        cosine = jnp.concatenate([cos_ref[...]] * (size // pt), axis=0)
        sine = jnp.concatenate([sin_ref[...]] * (size // pt), axis=0)
        x = x_ref[pl.ds(pl.multiple_of(base + low, pt), size)]
        mid, q, k, v = advance(
            x, mix_ref[pl.ds(low, size)], wo_ref, tq_ref, tk_ref, tv_ref, cosine, sine
        )
        mid_ref[pl.ds(low, size)] = mid
        for i in range(size // pt):
            for h in range(2):
                for n, a in enumerate((q, k, v)):
                    send_ref[2 * (low // pt + i) + h, :, n * half : (n + 1) * half] = a[
                        i * pt : (i + 1) * pt, h * half : (h + 1) * half
                    ]

    @pl.when(far > 0)
    def _():
        gather, spread = head_maps(inner)
        own_spot = jnp.where(first, 0, REACH)
        for j in range(REACH):

            @pl.when(j < far)
            def _():
                spot = pl.ds(pl.multiple_of(jnp.where(first, REACH - 1 - j, j) * pt, pt), pt)
                norm = normed(far_ref[spot])
                fk_ref[j * pt : (j + 1) * pt] = dot(norm, wk_ref[...]).astype(BF16)
                fv_ref[j * pt : (j + 1) * pt] = dot(norm, wv_ref[...]).astype(BF16)

        for j in range(REACH):

            @pl.when(j < near)
            def _():
                spots = []
                for i in range(REACH):
                    at = own_spot + jnp.where(first, i, own - 1 - i)
                    spots.append(pl.ds(pl.multiple_of(at * pt, pt), pt))
                two, three = far >= 2, far >= 3
                keys, values = [], []
                for ref, own_ref, into in ((fk_ref, k_ref, keys), (fv_ref, v_ref, values)):
                    into.append(ref[0:pt])
                    into.append(jnp.where(two, ref[pt : 2 * pt], own_ref[spots[2]]))
                    into.append(jnp.where(three, ref[2 * pt : 3 * pt], own_ref[spots[1]]))
                    into.append(own_ref[spots[0]])
                same = [far >= 1, two | (near >= 3), three | (near >= 2), near >= 1]
                q = q_ref[pl.ds(pl.multiple_of(base + lows[j], pt), pt)]
                mix_ref[pl.ds(lows[j], pt)] = attend(q, keys, values, same, gather, spread)

        @pl.when((near == 1) & first)
        def _():
            finish(0, pt)

        @pl.when((near == 1) & jnp.logical_not(first))
        def _():
            finish(halo - pt, pt)

        @pl.when(near > 1)
        def _():
            finish(0, halo)

        def copies(j):
            slot = jnp.where(first, j, own - 1 - j)
            block = jnp.where(first, j, REACH - 1 - j)
            row = pl.ds(pl.multiple_of(slot * pt, pt), pt)
            return (
                pltpu.make_async_copy(mid_ref.at[pl.ds(lows[j], pt)], mid_out.at[row], sems.at[j, 0]),
                pltpu.make_async_copy(
                    send_ref.at[pl.ds(2 * block, 2)], send_out.at[pl.ds(2 * slot, 2)], sems.at[j, 1]
                ),
            )

        for j in range(REACH):

            @pl.when(j < near)
            def _():
                for c in copies(j):
                    c.start()

        for j in range(REACH):

            @pl.when(j < near)
            def _():
                for c in copies(j):
                    c.wait()


def time_kernel(in_ref, out_ref, v_ref):
    blocks, pt, width = in_ref.shape
    half = width // 3
    heads = half // HEAD_DIM
    k = in_ref[:, :, half : 2 * half].reshape(blocks * pt, half)
    v = in_ref[:, :, 2 * half :].reshape(blocks * pt, half)
    keeps = [lax.broadcasted_iota(jnp.int32, (1, half), 1) // HEAD_DIM == h for h in range(heads)]
    for h in range(heads):
        v_ref[h] = jnp.where(keeps[h], v, jnp.ones_like(v))
    step = 2
    for at in range(0, blocks, step):
        q = in_ref[at : at + step, :, :half].reshape(step * pt, half)
        out = jnp.zeros((step * pt, half), F32)
        for h in range(heads):
            scores = lax.dot_general(
                jnp.where(keeps[h], q, jnp.zeros_like(q)), k, (((1,), (1,)), ((), ())),
                preferred_element_type=F32,
            )
            weights = jnp.exp(scores - jnp.max(scores, axis=-1, keepdims=True)).astype(BF16)
            both = dot(weights, v_ref[h])
            out = jnp.where(keeps[h], both / pltpu.roll(both, half // 2, 1), out)
        out_ref[at : at + step] = out.reshape(step, pt, half).astype(BF16)


def out_kernel(mixed_ref, mid_ref, wo_ref, out_hbm, out_ref, sems):
    blocks, pt, half = mixed_ref.shape
    copies = []
    for s in range(blocks // 2):
        part = pl.ds(s * pt, pt)
        mixed = jnp.concatenate([mixed_ref[2 * s], mixed_ref[2 * s + 1]], axis=1)
        out_ref[part] = (mid_ref[part].astype(F32) + dot(mixed, wo_ref[...])).astype(BF16)
        copies.append(pltpu.make_async_copy(out_ref.at[part], out_hbm.at[part], sems.at[s]))
        copies[-1].start()
    for c in copies:
        c.wait()


def params(mib=32):
    return pltpu.CompilerParams(vmem_limit_bytes=mib << 20)


def cost(flops, moved):
    return pl.CostEstimate(flops=flops, bytes_accessed=moved, transcendentals=0)


def shape(*dims):
    return jax.ShapeDtypeStruct(dims, BF16)


def on_device(
    series_data, group_ids, group_query, group_key, group_value, group_out,
    time_query, time_key, time_value, time_out,
):
    s_dev, pt, feature = series_data.shape
    inner = group_query.shape[1]
    rows, halo = s_dev * pt, REACH * pt
    x = series_data.reshape(rows, feature)
    swaps = []
    for i in range(1, lax.axis_size(SERIES) - 1, 2):
        swaps += [(i, i + 1), (i + 1, i)]
    to_far = pl.pallas_call(
        cut_kernel,
        out_shape=shape(halo, feature),
        in_specs=[HBM],
        out_specs=VMEM,
        scratch_shapes=[pltpu.SemaphoreType.DMA((6,))],
        compiler_params=params(62),
        cost_estimate=cost(0, 2 << 20),
        name="cut",
    )(x)
    to_far, x = lax.optimization_barrier((to_far, x))
    far = lax.ppermute(to_far, SERIES, swaps)
    pair = lax.ppermute(x, "core", [(0, 1), (1, 0)])

    positions = lax.axis_index(TIME) * pt + jnp.arange(pt, dtype=jnp.int32)
    halfway = HEAD_DIM // 2
    freqs = 10000.0 ** (-jnp.arange(halfway, dtype=F32) / halfway)
    angles = positions.astype(F32)[:, None] * freqs[None, :]
    cosine, sine = jnp.cos(angles), jnp.sin(angles)
    cosine = jnp.concatenate([cosine] * 4, axis=1)
    sine = jnp.concatenate([-sine, sine, -sine, sine], axis=1)
    weights = (group_query, group_key, group_value, group_out, time_query, time_key, time_value)
    mid_shape, send_shape = shape(rows, feature), shape(2 * s_dev, pt, 3 * inner // 2)
    q, k, v, mid, send, *loaded = pl.pallas_call(
        own_kernel,
        out_shape=[shape(rows, inner)] + [shape(rows + halo, inner)] * 2 + [mid_shape, send_shape]
        + [shape(*w.shape) for w in weights[1:]],
        in_specs=[SMEM] + [VMEM] * 2 + [HBM] * 7 + [VMEM] * 2,
        out_specs=[VMEM] * 11,
        scratch_shapes=[
            pltpu.VMEM((rows, inner), BF16),
            pltpu.VMEM(group_query.shape, BF16),
            pltpu.SemaphoreType.DMA((7, 2)),
        ],
        compiler_params=params(41),
        cost_estimate=cost(2 * feature * inner * (7 * rows + 2 * halo), 16 << 20),
        name="own",
    )(group_ids, x, pair, *weights, cosine, sine)
    mid, send = pl.pallas_call(
        fix_kernel,
        out_shape=[mid_shape, send_shape],
        in_specs=[SMEM] + [VMEM] * 13 + [ANY] * 2,
        out_specs=[ANY] * 2,
        scratch_shapes=[
            pltpu.VMEM((halo, inner), BF16),
            pltpu.VMEM((halo, inner), BF16),
            pltpu.VMEM((halo, inner), BF16),
            pltpu.VMEM((halo, feature), BF16),
            pltpu.VMEM((2 * REACH, pt, 3 * inner // 2), BF16),
        ]
        + [pltpu.SemaphoreType.DMA((REACH, 2))],
        input_output_aliases={14: 0, 15: 1},
        compiler_params=params(),
        cost_estimate=cost(2 * feature * inner * 7 * pt, 4 << 20),
        name="fix",
    )(group_ids, far, x, q, k, v, *loaded, cosine, sine, mid, send)

    got = lax.all_to_all(send, TIME, split_axis=0, concat_axis=0, tiled=True)
    mixed = pl.pallas_call(
        time_kernel,
        out_shape=shape(2 * s_dev, pt, inner // 2),
        in_specs=[VMEM],
        out_specs=VMEM,
        scratch_shapes=[pltpu.VMEM((HEADS // 2, 2 * s_dev * pt, inner // 2), BF16)],
        compiler_params=params(),
        cost_estimate=cost(8 << 30, 2 << 20),
        name="time",
    )(got)
    back = lax.all_to_all(mixed, TIME, split_axis=0, concat_axis=0, tiled=True)
    out = pl.pallas_call(
        out_kernel,
        out_shape=shape(rows, feature),
        in_specs=[VMEM] * 3,
        out_specs=HBM,
        scratch_shapes=[pltpu.VMEM((rows, feature), BF16), pltpu.SemaphoreType.DMA((s_dev,))],
        compiler_params=params(),
        cost_estimate=cost(2 * feature * inner * rows, 4 << 20),
        name="out",
    )(back, mid, time_out)
    return out.reshape(s_dev, pt, feature)


def solution(mesh):
    names = ("zh", "x", "core", "zl", "y")
    fine = Mesh(mesh.devices.reshape(4, 4, 2, 2, 4), names)
    whole = P(SERIES, TIME, None)
    placed = (whole,) + (P(),) * 9
    return jax.shard_map(
        on_device, mesh=fine, in_specs=placed, out_specs=whole, check_vma=False
    )
```

```python
import functools

import jax
import jax.numpy as jnp
from jax import lax
from jax.experimental import pallas as pl
from jax.experimental.pallas import tpu as pltpu
from jax.sharding import Mesh, PartitionSpec as P

HEADS = 8
HEAD_DIM = 64
REACH = 3
GROUP = 1
BF16 = jnp.bfloat16
F32 = jnp.float32
SERIES = ("zh", "x", "core")
TIME = ("zl", "y")
VMEM = pl.BlockSpec(memory_space=pltpu.VMEM)
ANY = pl.BlockSpec(memory_space=pl.ANY)
HBM = pl.BlockSpec(memory_space=pltpu.HBM)
SMEM = pl.BlockSpec(memory_space=pltpu.SMEM)


def dot(a, b):
    return jnp.dot(a, b, preferred_element_type=F32)


def normed(values):
    wide = values.astype(F32)
    return (wide * lax.rsqrt(jnp.mean(wide * wide, axis=-1, keepdims=True) + 1e-06)).astype(BF16)


def cut_kernel(x_hbm, far_ref, sems):
    rows, halo = x_hbm.shape[0], far_ref.shape[0]
    pt = rows - halo
    first = pl.multiple_of(jnp.where(lax.axis_index("core") == 0, 0, pt), pt)
    step = halo // sems.shape[0]
    copies = [
        pltpu.make_async_copy(
            x_hbm.at[pl.ds(first + i * step, step)], far_ref.at[pl.ds(i * step, step)], sems.at[i]
        )
        for i in range(sems.shape[0])
    ]
    for c in copies:
        c.start()
    for c in copies:
        c.wait()


def head_maps(inner):
    row = lax.broadcasted_iota(jnp.int32, (inner, 128), 0)
    col = lax.broadcasted_iota(jnp.int32, (inner, 128), 1)
    gather = (row // HEAD_DIM == col).astype(BF16)
    row = lax.broadcasted_iota(jnp.int32, (128, inner), 0)
    col = lax.broadcasted_iota(jnp.int32, (128, inner), 1)
    return gather, (col // HEAD_DIM == row).astype(BF16)


def attend(series, gather, spread):
    pt = series[0][0].shape[0]
    span = len(series[0][1])
    prods = [q * k for q, keys, _, _ in series for k in keys]
    scores = dot(jnp.concatenate(prods, axis=0), gather)
    shares = []
    for i, (_, _, _, same) in enumerate(series):
        parts = [
            jnp.where(m, scores[(i * span + j) * pt : (i * span + j + 1) * pt], -1e30)
            for j, m in enumerate(same)
        ]
        top = functools.reduce(jnp.maximum, parts)
        weights = [jnp.exp(p - top) for p in parts]
        inverse = 1.0 / functools.reduce(jnp.add, weights)
        shares += [(w * inverse).astype(BF16) for w in weights]
    wide = dot(jnp.concatenate(shares, axis=0), spread)
    out = []
    for i, (_, _, values, _) in enumerate(series):
        total = jnp.zeros(values[0].shape, F32)
        for j, v in enumerate(values):
            total += wide[(i * span + j) * pt : (i * span + j + 1) * pt] * v.astype(F32)
        out.append(total.astype(BF16))
    return out


def turn(values, cosine, sine):
    lane = lax.broadcasted_iota(jnp.int32, cosine.shape, 1)
    low = lane % HEAD_DIM < HEAD_DIM // 2
    out = []
    for at in range(0, values.shape[1], 128):
        v = values[:, at : at + 128]
        swapped = jnp.where(low, pltpu.roll(v, 96, 1), pltpu.roll(v, 32, 1))
        out.append(v * cosine + swapped * sine)
    return jnp.concatenate(out, axis=1)


def advance(x, mixed, wo_ref, tq_ref, tk_ref, tv_ref, cosine, sine):
    mid = (x.astype(F32) + dot(mixed, wo_ref[...])).astype(BF16)
    norm = normed(mid)
    q = (turn(dot(norm, tq_ref[...]), cosine, sine) * HEAD_DIM ** -0.5).astype(BF16)
    k = turn(dot(norm, tk_ref[...]), cosine, sine).astype(BF16)
    return mid, q, k, dot(norm, tv_ref[...]).astype(BF16)


def fetch(source, target, sems):
    rows = source.shape[0] // 2
    parts = [pl.ds(n * rows, rows) for n in range(2)]
    return [pltpu.make_async_copy(source.at[p], target.at[p], sems.at[n]) for n, p in enumerate(parts)]


def start(*copies):
    for c in copies:
        c.start()


def wait(*copies):
    for c in copies:
        c.wait()


def own_kernel(
    ids_ref, x_ref, pair_ref, wq_hbm, wk_hbm, wv_hbm, wo_hbm, tq_hbm, tk_hbm, tv_hbm, cos_ref, sin_ref,
    q_ref, k_ref, v_ref, mid_ref, send_ref, wk_ref, wv_ref, wo_ref, tq_ref, tk_ref, tv_ref,
    mix_ref, norm_ref, wq_ref, sems,
):
    sources = (wq_hbm, wk_hbm, wv_hbm, wo_hbm, tq_hbm, tk_hbm, tv_hbm)
    targets = (wq_ref, wk_ref, wv_ref, wo_ref, tq_ref, tk_ref, tv_ref)
    weights = [fetch(a, b, sems.at[i]) for i, (a, b) in enumerate(zip(sources, targets))]
    for w in weights:
        start(*w)
    pt, rows, inner = cos_ref.shape[0], x_ref.shape[0], q_ref.shape[1]
    own, halo = rows // pt, REACH * pt
    first = lax.axis_index("core") == 0
    own_spot = jnp.where(first, 0, REACH)
    pair_row = pl.multiple_of(jnp.where(first, rows, 0), pt)
    own_row = pl.multiple_of(own_spot * pt, pt)
    step = 2 * pt
    source = pl.multiple_of(jnp.where(first, 0, pt), pt)
    for at in range(0, rows, step):
        norm_ref[pl.ds(at, step)] = normed(x_ref[pl.ds(at, step)])
    norm_ref[pl.ds(rows, halo)] = normed(pair_ref[pl.ds(source, halo)])
    for n, (w_ref, to_ref) in enumerate(((wq_ref, q_ref), (wk_ref, k_ref), (wv_ref, v_ref))):
        wait(*weights[n])
        for at in range(0, rows, step):
            values = dot(norm_ref[pl.ds(at, step)], w_ref[...])
            if n == 0:
                to_ref[pl.ds(at, step)] = (values * HEAD_DIM ** -0.5).astype(BF16)
            else:
                to_ref[pl.ds(pl.multiple_of(own_row + at, pt), step)] = values.astype(BF16)
        if n > 0:
            to_ref[pl.ds(pair_row, halo)] = dot(norm_ref[pl.ds(rows, halo)], w_ref[...]).astype(BF16)
    gather, spread = head_maps(inner)
    span, count = REACH + 1, ids_ref.shape[0]
    place = lax.axis_index(SERIES) * own
    series = []
    for s in range(own):
        index = place + s
        mine = ids_ref[index]
        back = jnp.int32(0)
        for j in range(1, span):
            back += ((ids_ref[jnp.maximum(index - j, 0)] == mine) & (index >= j)).astype(jnp.int32)
        base = jnp.clip(own_spot + s - back, 0, REACH)
        spots = [pl.ds(pl.multiple_of((base + j) * pt, pt), pt) for j in range(span)]
        others = [place - own_spot + base + j for j in range(span)]
        same = [
            (ids_ref[jnp.clip(o, 0, count - 1)] == mine) & (o >= 0) & (o < count) for o in others
        ]
        series.append(
            (q_ref[s * pt : (s + 1) * pt], [k_ref[p] for p in spots], [v_ref[p] for p in spots], same)
        )
    for s in range(0, own, GROUP):
        for i, mixed in enumerate(attend(series[s : s + GROUP], gather, spread)):
            mix_ref[(s + i) * pt : (s + i + 1) * pt] = mixed
    for w in weights[3:]:
        wait(*w)
    half = inner // 2
    cosine = jnp.concatenate([cos_ref[...]] * 2, axis=0)
    sine = jnp.concatenate([sin_ref[...]] * 2, axis=0)
    for at in range(0, rows, step):
        part = pl.ds(at, step)
        mid, q, k, v = advance(x_ref[part], mix_ref[part], wo_ref, tq_ref, tk_ref, tv_ref, cosine, sine)
        mid_ref[part] = mid
        for i in range(2):
            for h in range(2):
                for n, a in enumerate((q, k, v)):
                    send_ref[2 * (at // pt + i) + h, :, n * half : (n + 1) * half] = a[
                        i * pt : (i + 1) * pt, h * half : (h + 1) * half
                    ]


def fix_kernel(
    ids_ref, far_ref, x_ref, q_ref, k_ref, v_ref, wk_ref, wv_ref, wo_ref, tq_ref, tk_ref, tv_ref,
    cos_ref, sin_ref, mid_in, send_in,
    mid_ref, send_ref,
    fk_ref, fv_ref,
):
    del mid_in, send_in
    pt, rows, inner = cos_ref.shape[0], x_ref.shape[0], q_ref.shape[1]
    own, count, half = rows // pt, ids_ref.shape[0], inner // 2
    first = lax.axis_index("core") == 0
    place = lax.axis_index(SERIES) * own
    border = jnp.where(first, place, place + own - 1)
    way = jnp.where(first, -1, 1)
    mine = ids_ref[border]

    def run(at, step):
        size = jnp.int32(0)
        for j in range(REACH):
            spot = at + j * step
            size += (
                (spot >= 0) & (spot < count) & (ids_ref[jnp.clip(spot, 0, count - 1)] == mine)
            ).astype(jnp.int32)
        return size

    far = run(border + way, way)
    near = run(border, -way)

    def block(index, size=1):
        return pl.ds(pl.multiple_of(index * pt, pt), size * pt)

    for n in range(1, REACH + 1):

        @pl.when(far == n)
        def _():
            spot = block(jnp.where(first, REACH - n, 0), n)
            norm = normed(far_ref[spot])
            fk_ref[spot] = dot(norm, wk_ref[...]).astype(BF16)
            fv_ref[spot] = dot(norm, wv_ref[...]).astype(BF16)

    for n in range(1, REACH + 1):

        @pl.when((far > 0) & (near == n))
        def _():
            gather, spread = head_maps(inner)
            fars = [block(jnp.where(first, REACH - 1 - j, j)) for j in range(REACH)]
            nears = [block(jnp.where(first, j, REACH + own - 1 - j)) for j in range(n)]

            def candidates(halo_ref, own_ref):
                if n == 1:
                    return [halo_ref[spot] for spot in fars] + [own_ref[nears[0]]]
                if n == 2:
                    return [halo_ref[spot] for spot in fars[:2]] + [own_ref[spot] for spot in nears]
                return [halo_ref[fars[0]]] + [own_ref[spot] for spot in nears]

            same = [far > j for j in range(REACH + 1 - n)] + [far > 0] * n
            keys, values = candidates(fk_ref, k_ref), candidates(fv_ref, v_ref)
            slot = jnp.where(first, 0, own - n)
            queries = [q_ref[block(slot + i)] for i in range(n)]
            mixed = attend([(q, keys, values, same) for q in queries], gather, spread)
            mid, q, k, v = advance(
                x_ref[block(slot, n)], jnp.concatenate(mixed, axis=0), wo_ref, tq_ref, tk_ref, tv_ref,
                jnp.concatenate([cos_ref[...]] * n, axis=0), jnp.concatenate([sin_ref[...]] * n, axis=0),
            )
            mid_ref[block(slot, n)] = mid
            for i in range(n):
                for h in range(2):
                    for m, a in enumerate((q, k, v)):
                        send_ref[2 * (slot + i) + h, :, m * half : (m + 1) * half] = a[
                            i * pt : (i + 1) * pt, h * half : (h + 1) * half
                        ]


def time_kernel(in_ref, out_ref, v_ref):
    blocks, pt, width = in_ref.shape
    half = width // 3
    heads = half // HEAD_DIM
    k = in_ref[:, :, half : 2 * half].reshape(blocks * pt, half)
    v = in_ref[:, :, 2 * half :].reshape(blocks * pt, half)
    keeps = [lax.broadcasted_iota(jnp.int32, (1, half), 1) // HEAD_DIM == h for h in range(heads)]
    for h in range(heads):
        v_ref[h] = jnp.where(keeps[h], v, jnp.ones_like(v))
    step = 2
    for at in range(0, blocks, step):
        q = in_ref[at : at + step, :, :half].reshape(step * pt, half)
        out = jnp.zeros((step * pt, half), F32)
        for h in range(heads):
            scores = lax.dot_general(
                jnp.where(keeps[h], q, jnp.zeros_like(q)), k, (((1,), (1,)), ((), ())),
                preferred_element_type=F32,
            )
            weights = jnp.exp((scores - jnp.max(scores, axis=-1, keepdims=True)).astype(BF16))
            both = dot(weights, v_ref[h])
            out = jnp.where(keeps[h], both / pltpu.roll(both, half // 2, 1), out)
        out_ref[at : at + step] = out.reshape(step, pt, half).astype(BF16)


def out_kernel(mixed_ref, mid_ref, wo_ref, out_hbm, out_ref, sems):
    blocks, pt, half = mixed_ref.shape
    copies = []
    for s in range(blocks // 2):
        part = pl.ds(s * pt, pt)
        mixed = jnp.concatenate([mixed_ref[2 * s], mixed_ref[2 * s + 1]], axis=1)
        out_ref[part] = (mid_ref[part].astype(F32) + dot(mixed, wo_ref[...])).astype(BF16)
        copies.append(pltpu.make_async_copy(out_ref.at[part], out_hbm.at[part], sems.at[s]))
        copies[-1].start()
    for c in copies:
        c.wait()


def params(mib=32):
    return pltpu.CompilerParams(vmem_limit_bytes=mib << 20)


def cost(flops, moved):
    return pl.CostEstimate(flops=flops, bytes_accessed=moved, transcendentals=0)


def shape(*dims):
    return jax.ShapeDtypeStruct(dims, BF16)


def in_vmem(*dims):
    return pltpu.VMEM(dims, BF16)


def in_hbm(array):
    return pltpu.with_memory_space_constraint(array, pltpu.HBM)


def on_device(
    series_data, group_ids, group_query, group_key, group_value, group_out,
    time_query, time_key, time_value, time_out,
):
    s_dev, pt, feature = series_data.shape
    inner = group_query.shape[1]
    rows, halo = s_dev * pt, REACH * pt
    x = series_data.reshape(rows, feature)
    swaps = []
    for i in range(1, lax.axis_size(SERIES) - 1, 2):
        swaps += [(i, i + 1), (i + 1, i)]
    to_far = pl.pallas_call(
        cut_kernel,
        out_shape=shape(halo, feature),
        in_specs=[HBM],
        out_specs=VMEM,
        scratch_shapes=[pltpu.SemaphoreType.DMA((6,))],
        compiler_params=params(),
        cost_estimate=cost(0, 2 << 20),
        name="cut",
    )(in_hbm(x))
    far = lax.ppermute(to_far, SERIES, swaps)
    pair = lax.ppermute(x, "core", [(0, 1), (1, 0)])

    positions = lax.axis_index(TIME) * pt + jnp.arange(pt, dtype=jnp.int32)
    halfway = HEAD_DIM // 2
    freqs = 10000.0 ** (-jnp.arange(halfway, dtype=F32) / halfway)
    angles = positions.astype(F32)[:, None] * freqs[None, :]
    cosine, sine = jnp.cos(angles), jnp.sin(angles)
    cosine = jnp.concatenate([cosine] * 4, axis=1)
    sine = jnp.concatenate([-sine, sine, -sine, sine], axis=1)
    weights = (group_query, group_key, group_value, group_out, time_query, time_key, time_value)
    mid_shape, send_shape = in_vmem(rows, feature), in_vmem(2 * s_dev, pt, 3 * inner // 2)
    q, k, v, mid, send, *loaded = pl.pallas_call(
        own_kernel,
        out_shape=[in_vmem(rows, inner)] + [in_vmem(rows + halo, inner)] * 2 + [mid_shape, send_shape]
        + [in_vmem(*w.shape) for w in weights[1:]],
        in_specs=[SMEM] + [VMEM] * 2 + [HBM] * 7 + [VMEM] * 2,
        out_specs=[VMEM] * 11,
        scratch_shapes=[
            pltpu.VMEM((rows, inner), BF16),
            pltpu.VMEM((rows + halo, feature), BF16),
            pltpu.VMEM(group_query.shape, BF16),
            pltpu.SemaphoreType.DMA((7, 2)),
        ],
        compiler_params=params(40),
        cost_estimate=cost(2 * feature * inner * (7 * rows + 2 * halo), 16 << 20),
        name="own",
    )(group_ids, x, pair, *map(in_hbm, weights), cosine, sine)
    mid, send = pl.pallas_call(
        fix_kernel,
        out_shape=[mid_shape, send_shape],
        in_specs=[SMEM] + [VMEM] * 15,
        out_specs=[VMEM] * 2,
        scratch_shapes=[pltpu.VMEM((halo, inner), BF16)] * 2,
        input_output_aliases={14: 0, 15: 1},
        compiler_params=params(),
        cost_estimate=cost(2 * feature * inner * 7 * pt, 4 << 20),
        name="fix",
    )(group_ids, far, x, q, k, v, *loaded, cosine, sine, mid, send)

    got = lax.all_to_all(send, TIME, split_axis=0, concat_axis=0, tiled=True)
    mixed = pl.pallas_call(
        time_kernel,
        out_shape=shape(2 * s_dev, pt, inner // 2),
        in_specs=[VMEM],
        out_specs=VMEM,
        scratch_shapes=[pltpu.VMEM((HEADS // 2, 2 * s_dev * pt, inner // 2), BF16)],
        compiler_params=params(),
        cost_estimate=cost(8 << 30, 2 << 20),
        name="time",
    )(got)
    back = lax.all_to_all(mixed, TIME, split_axis=0, concat_axis=0, tiled=True)
    out = pl.pallas_call(
        out_kernel,
        out_shape=shape(rows, feature),
        in_specs=[VMEM] * 3,
        out_specs=HBM,
        scratch_shapes=[pltpu.VMEM((rows, feature), BF16), pltpu.SemaphoreType.DMA((s_dev,))],
        compiler_params=params(),
        cost_estimate=cost(2 * feature * inner * rows, 4 << 20),
        name="out",
    )(back, mid, time_out)
    return out.reshape(s_dev, pt, feature)


def solution(mesh):
    names = ("zh", "x", "core", "zl", "y")
    fine = Mesh(mesh.devices.reshape(4, 4, 2, 2, 4), names)
    whole = P(SERIES, TIME, None)
    placed = (whole,) + (P(),) * 9
    return jax.shard_map(
        on_device, mesh=fine, in_specs=placed, out_specs=whole, check_vma=False
    )
```

```python
import functools

import jax
import jax.numpy as jnp
from jax import lax
from jax.experimental import pallas as pl
from jax.experimental.pallas import tpu as pltpu
from jax.sharding import Mesh, PartitionSpec as P

HEADS = 8
HEAD_DIM = 64
REACH = 3
GROUP = 1
BF16 = jnp.bfloat16
F32 = jnp.float32
SERIES = ("zh", "x", "core")
TIME = ("zl", "y")
VMEM = pl.BlockSpec(memory_space=pltpu.VMEM)
ANY = pl.BlockSpec(memory_space=pl.ANY)
HBM = pl.BlockSpec(memory_space=pltpu.HBM)
SMEM = pl.BlockSpec(memory_space=pltpu.SMEM)


def dot(a, b):
    return jnp.dot(a, b, preferred_element_type=F32)


def normed(values):
    wide = values.astype(F32)
    return (wide * lax.rsqrt(jnp.mean(wide * wide, axis=-1, keepdims=True) + 1e-06)).astype(BF16)


def cut_kernel(x_hbm, far_ref, sems):
    rows, halo = x_hbm.shape[0], far_ref.shape[0]
    pt = rows - halo
    first = pl.multiple_of(jnp.where(lax.axis_index("core") == 0, 0, pt), pt)
    step = halo // sems.shape[0]
    copies = [
        pltpu.make_async_copy(
            x_hbm.at[pl.ds(first + i * step, step)], far_ref.at[pl.ds(i * step, step)], sems.at[i]
        )
        for i in range(sems.shape[0])
    ]
    for c in copies:
        c.start()
    for c in copies:
        c.wait()


def head_maps(inner):
    row = lax.broadcasted_iota(jnp.int32, (inner, 128), 0)
    col = lax.broadcasted_iota(jnp.int32, (inner, 128), 1)
    gather = (row // HEAD_DIM == col).astype(BF16)
    row = lax.broadcasted_iota(jnp.int32, (128, inner), 0)
    col = lax.broadcasted_iota(jnp.int32, (128, inner), 1)
    return gather, (col // HEAD_DIM == row).astype(BF16)


def attend(series, gather, spread):
    pt = series[0][0].shape[0]
    span = len(series[0][1])
    prods = [q * k for q, keys, _, _ in series for k in keys]
    scores = dot(jnp.concatenate(prods, axis=0), gather)
    shares = []
    for i, (_, _, _, same) in enumerate(series):
        parts = [
            jnp.where(m, scores[(i * span + j) * pt : (i * span + j + 1) * pt], -1e30)
            for j, m in enumerate(same)
        ]
        top = functools.reduce(jnp.maximum, parts)
        weights = [jnp.exp(p - top) for p in parts]
        inverse = 1.0 / functools.reduce(jnp.add, weights)
        shares += [(w * inverse).astype(BF16) for w in weights]
    wide = dot(jnp.concatenate(shares, axis=0), spread)
    out = []
    for i, (_, _, values, _) in enumerate(series):
        total = jnp.zeros(values[0].shape, F32)
        for j, v in enumerate(values):
            total += wide[(i * span + j) * pt : (i * span + j + 1) * pt] * v.astype(F32)
        out.append(total.astype(BF16))
    return out


def turn(values, cosine, sine):
    lane = lax.broadcasted_iota(jnp.int32, cosine.shape, 1)
    low = lane % HEAD_DIM < HEAD_DIM // 2
    out = []
    for at in range(0, values.shape[1], 128):
        v = values[:, at : at + 128]
        swapped = jnp.where(low, pltpu.roll(v, 96, 1), pltpu.roll(v, 32, 1))
        out.append(v * cosine + swapped * sine)
    return jnp.concatenate(out, axis=1)


def advance(x, mixed, wo_ref, tq_ref, tk_ref, tv_ref, cosine, sine):
    mid = (x.astype(F32) + dot(mixed, wo_ref[...])).astype(BF16)
    norm = normed(mid)
    q = (turn(dot(norm, tq_ref[...]), cosine, sine) * HEAD_DIM ** -0.5).astype(BF16)
    k = turn(dot(norm, tk_ref[...]), cosine, sine).astype(BF16)
    return mid, q, k, dot(norm, tv_ref[...]).astype(BF16)


def fetch(source, target, sems):
    rows = source.shape[0] // 2
    parts = [pl.ds(n * rows, rows) for n in range(2)]
    return [pltpu.make_async_copy(source.at[p], target.at[p], sems.at[n]) for n, p in enumerate(parts)]


def start(*copies):
    for c in copies:
        c.start()


def wait(*copies):
    for c in copies:
        c.wait()


def own_kernel(
    ids_ref, x_ref, pair_ref, wq_hbm, wk_hbm, wv_hbm, wo_hbm, tq_hbm, tk_hbm, tv_hbm, cos_ref, sin_ref,
    q_ref, k_ref, v_ref, mid_ref, send_ref, wk_ref, wv_ref, wo_ref, tq_ref, tk_ref, tv_ref,
    mix_ref, norm_ref, wq_ref, sems,
):
    sources = (wq_hbm, wk_hbm, wv_hbm, wo_hbm, tq_hbm, tk_hbm, tv_hbm)
    targets = (wq_ref, wk_ref, wv_ref, wo_ref, tq_ref, tk_ref, tv_ref)
    weights = [fetch(a, b, sems.at[i]) for i, (a, b) in enumerate(zip(sources, targets))]
    for w in weights:
        start(*w)
    pt, rows, inner = cos_ref.shape[0], x_ref.shape[0], q_ref.shape[1]
    own, halo = rows // pt, REACH * pt
    first = lax.axis_index("core") == 0
    own_spot = jnp.where(first, 0, REACH)
    pair_row = pl.multiple_of(jnp.where(first, rows, 0), pt)
    own_row = pl.multiple_of(own_spot * pt, pt)
    step = 2 * pt
    source = pl.multiple_of(jnp.where(first, 0, pt), pt)
    for at in range(0, rows, step):
        norm_ref[pl.ds(at, step)] = normed(x_ref[pl.ds(at, step)])
    norm_ref[pl.ds(rows, halo)] = normed(pair_ref[pl.ds(source, halo)])
    for n, (w_ref, to_ref) in enumerate(((wq_ref, q_ref), (wk_ref, k_ref), (wv_ref, v_ref))):
        wait(*weights[n])
        for at in range(0, rows, step):
            values = dot(norm_ref[pl.ds(at, step)], w_ref[...])
            if n == 0:
                to_ref[pl.ds(at, step)] = (values * HEAD_DIM ** -0.5).astype(BF16)
            else:
                to_ref[pl.ds(pl.multiple_of(own_row + at, pt), step)] = values.astype(BF16)
        if n > 0:
            to_ref[pl.ds(pair_row, halo)] = dot(norm_ref[pl.ds(rows, halo)], w_ref[...]).astype(BF16)
    gather, spread = head_maps(inner)
    span, count = REACH + 1, ids_ref.shape[0]
    place = lax.axis_index(SERIES) * own
    series = []
    for s in range(own):
        index = place + s
        mine = ids_ref[index]
        back = jnp.int32(0)
        for j in range(1, span):
            back += ((ids_ref[jnp.maximum(index - j, 0)] == mine) & (index >= j)).astype(jnp.int32)
        base = jnp.clip(own_spot + s - back, 0, REACH)
        spots = [pl.ds(pl.multiple_of((base + j) * pt, pt), pt) for j in range(span)]
        others = [place - own_spot + base + j for j in range(span)]
        same = [
            (ids_ref[jnp.clip(o, 0, count - 1)] == mine) & (o >= 0) & (o < count) for o in others
        ]
        series.append(
            (q_ref[s * pt : (s + 1) * pt], [k_ref[p] for p in spots], [v_ref[p] for p in spots], same)
        )
    for s in range(0, own, GROUP):
        for i, mixed in enumerate(attend(series[s : s + GROUP], gather, spread)):
            mix_ref[(s + i) * pt : (s + i + 1) * pt] = mixed
    for w in weights[3:]:
        wait(*w)
    half = inner // 2
    cosine = jnp.concatenate([cos_ref[...]] * 2, axis=0)
    sine = jnp.concatenate([sin_ref[...]] * 2, axis=0)
    for at in range(0, rows, step):
        part = pl.ds(at, step)
        mid, q, k, v = advance(x_ref[part], mix_ref[part], wo_ref, tq_ref, tk_ref, tv_ref, cosine, sine)
        mid_ref[part] = mid
        for i in range(2):
            for h in range(2):
                for n, a in enumerate((q, k, v)):
                    send_ref[2 * (at // pt + i) + h, :, n * half : (n + 1) * half] = a[
                        i * pt : (i + 1) * pt, h * half : (h + 1) * half
                    ]


def fix_kernel(
    ids_ref, far_ref, x_ref, q_ref, k_ref, v_ref, wk_ref, wv_ref, wo_ref, tq_ref, tk_ref, tv_ref,
    cos_ref, sin_ref, mid_in, send_in,
    mid_ref, send_ref,
    fk_ref, fv_ref,
):
    del mid_in, send_in
    pt, rows, inner = cos_ref.shape[0], x_ref.shape[0], q_ref.shape[1]
    own, half = rows // pt, inner // 2
    first = lax.axis_index("core") == 0
    place = lax.axis_index(SERIES) * own
    spot = lax.broadcasted_iota(jnp.int32, ids_ref.shape, 1)
    ids = ids_ref[...].astype(F32)
    mine = jnp.sum(jnp.where(spot == jnp.where(first, place, place + own - 1), ids, 0.0))
    member = jnp.where(ids == mine, 1.0, 0.0)
    beyond = jnp.where(first, spot - place, place + own - 1 - spot) < 0
    here = (spot >= place) & (spot < place + own)
    far = jnp.sum(jnp.where(beyond, member, 0.0)).astype(jnp.int32)
    near = jnp.sum(jnp.where(here, member, 0.0)).astype(jnp.int32)

    def block(index, size=1):
        return pl.ds(pl.multiple_of(index * pt, pt), size * pt)

    for n in range(1, REACH + 1):

        @pl.when(far == n)
        def _():
            spot = block(jnp.where(first, REACH - n, 0), n)
            norm = normed(far_ref[spot])
            fk_ref[spot] = dot(norm, wk_ref[...]).astype(BF16)
            fv_ref[spot] = dot(norm, wv_ref[...]).astype(BF16)

    for n in range(1, REACH + 1):

        @pl.when((far > 0) & (near == n))
        def _():
            gather, spread = head_maps(inner)
            fars = [block(jnp.where(first, REACH - 1 - j, j)) for j in range(REACH)]
            nears = [block(jnp.where(first, j, REACH + own - 1 - j)) for j in range(n)]

            def candidates(halo_ref, own_ref):
                if n == 1:
                    return [halo_ref[spot] for spot in fars] + [own_ref[nears[0]]]
                if n == 2:
                    return [halo_ref[spot] for spot in fars[:2]] + [own_ref[spot] for spot in nears]
                return [halo_ref[fars[0]]] + [own_ref[spot] for spot in nears]

            same = [far > j for j in range(REACH + 1 - n)] + [far > 0] * n
            keys, values = candidates(fk_ref, k_ref), candidates(fv_ref, v_ref)
            slot = jnp.where(first, 0, own - n)
            queries = [q_ref[block(slot + i)] for i in range(n)]
            mixed = attend([(q, keys, values, same) for q in queries], gather, spread)
            mid, q, k, v = advance(
                x_ref[block(slot, n)], jnp.concatenate(mixed, axis=0), wo_ref, tq_ref, tk_ref, tv_ref,
                jnp.concatenate([cos_ref[...]] * n, axis=0), jnp.concatenate([sin_ref[...]] * n, axis=0),
            )
            mid_ref[block(slot, n)] = mid
            for i in range(n):
                for h in range(2):
                    for m, a in enumerate((q, k, v)):
                        send_ref[2 * (slot + i) + h, :, m * half : (m + 1) * half] = a[
                            i * pt : (i + 1) * pt, h * half : (h + 1) * half
                        ]


def time_kernel(in_ref, out_ref, v_ref):
    blocks, pt, width = in_ref.shape
    half = width // 3
    heads = half // HEAD_DIM
    k = in_ref[:, :, half : 2 * half].reshape(blocks * pt, half)
    v = in_ref[:, :, 2 * half :].reshape(blocks * pt, half)
    keeps = [lax.broadcasted_iota(jnp.int32, (1, half), 1) // HEAD_DIM == h for h in range(heads)]
    for h in range(heads):
        v_ref[h] = jnp.where(keeps[h], v, jnp.ones_like(v))
    step = 2
    for at in range(0, blocks, step):
        q = in_ref[at : at + step, :, :half].reshape(step * pt, half)
        out = jnp.zeros((step * pt, half), F32)
        for h in range(heads):
            scores = lax.dot_general(
                jnp.where(keeps[h], q, jnp.zeros_like(q)), k, (((1,), (1,)), ((), ())),
                preferred_element_type=F32,
            )
            weights = jnp.exp((scores - jnp.max(scores, axis=-1, keepdims=True)).astype(BF16))
            both = dot(weights, v_ref[h])
            out = jnp.where(keeps[h], both / pltpu.roll(both, half // 2, 1), out)
        out_ref[at : at + step] = out.reshape(step, pt, half).astype(BF16)


def out_kernel(mixed_ref, mid_ref, wo_ref, out_hbm, out_ref, sems):
    blocks, pt, half = mixed_ref.shape
    copies = []
    for s in range(blocks // 2):
        part = pl.ds(s * pt, pt)
        mixed = jnp.concatenate([mixed_ref[2 * s], mixed_ref[2 * s + 1]], axis=1)
        out_ref[part] = (mid_ref[part].astype(F32) + dot(mixed, wo_ref[...])).astype(BF16)
        copies.append(pltpu.make_async_copy(out_ref.at[part], out_hbm.at[part], sems.at[s]))
        copies[-1].start()
    for c in copies:
        c.wait()


def params(mib=32):
    return pltpu.CompilerParams(vmem_limit_bytes=mib << 20)


def cost(flops, moved):
    return pl.CostEstimate(flops=flops, bytes_accessed=moved, transcendentals=0)


def shape(*dims):
    return jax.ShapeDtypeStruct(dims, BF16)


def in_vmem(*dims):
    return pltpu.VMEM(dims, BF16)


def in_hbm(array):
    return pltpu.with_memory_space_constraint(array, pltpu.HBM)


def on_device(
    series_data, group_ids, group_query, group_key, group_value, group_out,
    time_query, time_key, time_value, time_out,
):
    s_dev, pt, feature = series_data.shape
    inner = group_query.shape[1]
    rows, halo = s_dev * pt, REACH * pt
    x = series_data.reshape(rows, feature)
    swaps = []
    for i in range(1, lax.axis_size(SERIES) - 1, 2):
        swaps += [(i, i + 1), (i + 1, i)]
    to_far = pl.pallas_call(
        cut_kernel,
        out_shape=shape(halo, feature),
        in_specs=[HBM],
        out_specs=VMEM,
        scratch_shapes=[pltpu.SemaphoreType.DMA((6,))],
        compiler_params=params(),
        cost_estimate=cost(0, 2 << 20),
        name="cut",
    )(in_hbm(x))
    far = lax.ppermute(to_far, SERIES, swaps)
    pair = lax.ppermute(x, "core", [(0, 1), (1, 0)])

    positions = lax.axis_index(TIME) * pt + jnp.arange(pt, dtype=jnp.int32)
    halfway = HEAD_DIM // 2
    freqs = 10000.0 ** (-jnp.arange(halfway, dtype=F32) / halfway)
    angles = positions.astype(F32)[:, None] * freqs[None, :]
    cosine, sine = jnp.cos(angles), jnp.sin(angles)
    cosine = jnp.concatenate([cosine] * 4, axis=1)
    sine = jnp.concatenate([-sine, sine, -sine, sine], axis=1)
    weights = (group_query, group_key, group_value, group_out, time_query, time_key, time_value)
    mid_shape, send_shape = in_vmem(rows, feature), in_vmem(2 * s_dev, pt, 3 * inner // 2)
    q, k, v, mid, send, *loaded = pl.pallas_call(
        own_kernel,
        out_shape=[in_vmem(rows, inner)] + [in_vmem(rows + halo, inner)] * 2 + [mid_shape, send_shape]
        + [in_vmem(*w.shape) for w in weights[1:]],
        in_specs=[SMEM] + [VMEM] * 2 + [HBM] * 7 + [VMEM] * 2,
        out_specs=[VMEM] * 11,
        scratch_shapes=[
            pltpu.VMEM((rows, inner), BF16),
            pltpu.VMEM((rows + halo, feature), BF16),
            pltpu.VMEM(group_query.shape, BF16),
            pltpu.SemaphoreType.DMA((7, 2)),
        ],
        compiler_params=params(40),
        cost_estimate=cost(2 * feature * inner * (7 * rows + 2 * halo), 16 << 20),
        name="own",
    )(group_ids, x, pair, *map(in_hbm, weights), cosine, sine)
    mid, send = pl.pallas_call(
        fix_kernel,
        out_shape=[mid_shape, send_shape],
        in_specs=[VMEM] * 16,
        out_specs=[VMEM] * 2,
        scratch_shapes=[pltpu.VMEM((halo, inner), BF16)] * 2,
        input_output_aliases={14: 0, 15: 1},
        compiler_params=params(),
        cost_estimate=cost(2 * feature * inner * 7 * pt, 4 << 20),
        name="fix",
    )(group_ids.reshape(1, -1), far, x, q, k, v, *loaded, cosine, sine, mid, send)

    got = lax.all_to_all(send, TIME, split_axis=0, concat_axis=0, tiled=True)
    mixed = pl.pallas_call(
        time_kernel,
        out_shape=shape(2 * s_dev, pt, inner // 2),
        in_specs=[VMEM],
        out_specs=VMEM,
        scratch_shapes=[pltpu.VMEM((HEADS // 2, 2 * s_dev * pt, inner // 2), BF16)],
        compiler_params=params(),
        cost_estimate=cost(8 << 30, 2 << 20),
        name="time",
    )(got)
    back = lax.all_to_all(mixed, TIME, split_axis=0, concat_axis=0, tiled=True)
    out = pl.pallas_call(
        out_kernel,
        out_shape=shape(rows, feature),
        in_specs=[VMEM] * 3,
        out_specs=HBM,
        scratch_shapes=[pltpu.VMEM((rows, feature), BF16), pltpu.SemaphoreType.DMA((s_dev,))],
        compiler_params=params(),
        cost_estimate=cost(2 * feature * inner * rows, 4 << 20),
        name="out",
    )(back, mid, time_out)
    return out.reshape(s_dev, pt, feature)


def solution(mesh):
    names = ("zh", "x", "core", "zl", "y")
    fine = Mesh(mesh.devices.reshape(4, 4, 2, 2, 4), names)
    whole = P(SERIES, TIME, None)
    placed = (whole,) + (P(),) * 9
    return jax.shard_map(
        on_device, mesh=fine, in_specs=placed, out_specs=whole, check_vma=False
    )
```
